1024 devices in a mesh: users: 64 (over z, x), items: 16 (over y, core).
Axes of the slice: x: 8, y: 8, z: 8, core: 2. Of those that a mesh axis runs over, the one named last changes fastest.
Arguments:
- confidence: bfloat16 [64, 16, 3, 512, 512], P('users', 'items'), may hold values from 1 to 30
- tile_block: int32 [64, 16, 3], P('users', 'items'), may hold values from 0 to 7, as said below
- tile_count: int32 [64, 16], P('users', 'items'), may hold values from 1 to 3, as said below
- item_factors: bfloat16 [65536, 256], P(('items', 'users')), may hold values from -4 to 4
Outputs:
- solution: float32 [32768, 256], P(('users', 'items'))
- residual: float32 [32768, 256], P(('users', 'items'))
The draws below stay inside these ranges and needn't reach their ends.
Inputs may be any that keep to these rules, and one draw needn't show every extreme that they name: `tile_block`: the live and the dead slots of one cell name different item blocks of its column. `tile_count`: some cell has all 3 slots live.
All inputs are finite; a program needn't handle non-finite values.
Results may differ from the reference program's by a relative error of at most 0.015.
Values may be sent and summed in bfloat16 or wider, within the bound.
No kernel may reach another device: no remote copies, remote signals or barrier semaphores. Data moves between devices by JAX's collectives and lax.ppermute only.
A program may use at most 32 MiB of HBM per device.

```python
import math
import jax
import jax.numpy as jnp
from jax import lax

RANK = 256
BLK = 512
IB_COL = 8
TPD = 3
STEPS = 2
NU = 32768
NI = 65536
N_USERS = 64
N_ITEMS = 16


def draw_tile_block(key, part):
    sub_key = jax.random.fold_in(key, 11)
    scores = jax.random.randint(sub_key, (N_USERS, N_ITEMS, IB_COL), 0, 1 << 20) * IB_COL
    scores = scores + jnp.arange(IB_COL, dtype=jnp.int32)
    order = jnp.argsort(scores, axis=-1).astype(jnp.int32)
    return order[:, :, :TPD]


def draw_tile_count(key, part):
    count_key = jax.random.fold_in(key, 13)
    pick_key = jax.random.fold_in(key, 17)
    counts = jax.random.randint(count_key, (N_USERS * N_ITEMS,), 1, TPD + 1)
    chosen = jax.random.randint(pick_key, (), 0, N_USERS * N_ITEMS)
    positions = jnp.arange(N_USERS * N_ITEMS, dtype=jnp.int32)
    counts = jnp.where(positions == chosen, TPD, counts)
    return counts.reshape(N_USERS, N_ITEMS).astype(jnp.int32)


def draw_item_factors(key, part):
    key = jax.random.fold_in(key, 23)
    value_key = jax.random.fold_in(key, 1)
    pick_key = jax.random.fold_in(key, 2)
    mean_key = jax.random.fold_in(key, 3)
    sign_key = jax.random.fold_in(key, 4)
    values = jnp.clip(jax.random.normal(value_key, (NI, RANK), jnp.float32), -4.0, 4.0)
    shared = 1.0
    group_rows = 64
    group_total = (NI + group_rows - 1) // group_rows
    means = jnp.clip(jax.random.normal(mean_key, (group_total, RANK), jnp.float32), -4.0, 4.0)
    spread_means = jnp.repeat(means, group_rows, axis=0)[:NI]
    signs = (jax.random.randint(sign_key, (NI,), 0, 2) * 2 - 1).astype(jnp.float32)
    values = (values + signs[:, None] * spread_means) * (1.0 + shared) ** (-0.5)
    values = jnp.clip(values, -4.0, 4.0)
    shard_rows = NI // (N_USERS * N_ITEMS)
    chosen = jax.random.randint(pick_key, (), 0, N_USERS * N_ITEMS)
    row_ids = jnp.arange(NI, dtype=jnp.int32) // shard_rows
    boost = jnp.where(row_ids == chosen, 6.0, 1.0).astype(jnp.float32)
    values = values * boost[:, None] * float(NI) ** (-0.5)
    return values.astype(jnp.bfloat16)


def levels(stream_key, extent, cuts, least, largest):
    loudness, own = 1.0, jax.random.fold_in(stream_key, 6)
    for axis_at, blocks in cuts:
        heights = jnp.exp(jax.random.uniform(jax.random.fold_in(own, axis_at), (blocks,), jnp.float32, least / len(cuts), largest / len(cuts)))
        loudness = loudness * jnp.repeat(heights, extent[axis_at] // blocks).reshape([-1 if axis == axis_at else 1 for axis in range(len(extent))])
    return loudness


def setup_inputs(seed: int = 0) -> dict:
    key_of = jax.random.split(jax.random.key(seed), 5)
    confidence = jnp.clip(jnp.exp(math.log(30.0) - 3.4011974 * jax.random.uniform(key_of[0], (N_USERS, N_ITEMS, TPD, BLK, BLK), jnp.float32) ** levels(key_of[0], (N_USERS, N_ITEMS, TPD, BLK, BLK), ((0, 64), (1, 16)), -0.2, 0.2)), 1.0, 30.0).astype(jnp.bfloat16)
    tile_block = draw_tile_block(jax.random.fold_in(key_of[4], 71), 0)
    tile_count = draw_tile_count(jax.random.fold_in(key_of[4], 71), 0)
    item_factors = draw_item_factors(jax.random.fold_in(key_of[4], 71), 0)
    return dict(confidence=confidence, tile_block=tile_block, tile_count=tile_count, item_factors=item_factors)


damping = 0.1


def reference(confidence, tile_block, tile_count, item_factors):
    gram = jnp.dot(item_factors.T, item_factors, preferred_element_type=jnp.float32)

    def row_solve(row_inputs):
        tile_values, block_ids, live_count = row_inputs
        flat_tiles = tile_values.reshape(N_ITEMS * TPD, BLK, BLK)
        owners = jnp.repeat(jnp.arange(N_ITEMS, dtype=jnp.int32), TPD)
        starts = ((owners * IB_COL + block_ids.reshape(-1)) * BLK).astype(jnp.int32)
        slot_ids = jnp.tile(jnp.arange(TPD, dtype=jnp.int32), N_ITEMS)
        live_flags = (slot_ids < jnp.repeat(live_count, TPD)).astype(jnp.float32)

        def tile_sum(left_rows):
            def accumulate(running, entry):
                tile, start, keep_flag = entry
                factors = lax.dynamic_slice_in_dim(item_factors, start, BLK, 0)
                values = tile.astype(jnp.float32)
                if left_rows is None:
                    weighted = (1.0 + values).astype(jnp.bfloat16)
                else:
                    scores = lax.dot_general(left_rows, factors, (((1,), (1,)), ((), ())), preferred_element_type=jnp.float32)
                    weighted = (values * scores).astype(jnp.bfloat16)
                term = jnp.dot(weighted, factors, preferred_element_type=jnp.float32)
                return running + keep_flag * term, None

            empty = jnp.zeros((BLK, RANK), jnp.float32)
            total, unused = lax.scan(accumulate, empty, (flat_tiles, starts, live_flags))
            return total

        def operator(direction):
            local = tile_sum(direction.astype(jnp.bfloat16))
            return local + jnp.dot(direction, gram, precision=lax.Precision.HIGHEST) + damping * direction

        right_side = tile_sum(None)
        solution = jnp.zeros_like(right_side)
        residual = right_side
        direction = right_side
        norm_now = jnp.sum(residual * residual, axis=1, keepdims=True)
        for step in range(STEPS):
            image = operator(direction)
            step_size = norm_now / jnp.sum(direction * image, axis=1, keepdims=True)
            solution = solution + step_size * direction
            residual = residual - step_size * image
            norm_next = jnp.sum(residual * residual, axis=1, keepdims=True)
            direction = residual + (norm_next / norm_now) * direction
            norm_now = norm_next
        return solution, residual

    solutions, residuals = lax.map(row_solve, (confidence, tile_block, tile_count))
    return solutions.reshape(NU, RANK), residuals.reshape(NU, RANK)
```

```python
import functools

import jax
import jax.numpy as jnp
from jax import lax
from jax.experimental import pallas as pl
from jax.experimental.pallas import tpu as pltpu
from jax.sharding import Mesh
from jax.sharding import PartitionSpec as P

STEPS = 2
DAMPING = 0.1
ROW_CHUNK = 256
VMEM_BYTES = 24 * 1024 * 1024
LANES = 128
SCALE_ROWS = 16
SCALE_STEPS = 64.0
FULL_SCALE = 32000.0
USERS = ("z", "x")
ITEMS = ("y", "core")


def tile_kernel(with_direction, count_ref, block_ref, tiles_ref, column_ref, *refs):
    if with_direction:
        left_ref, gram_ref, out_ref, total_ref = refs
    else:
        out_ref, total_ref = refs
    slot = pl.program_id(0)
    rows, rank = total_ref.shape

    @pl.when(slot == 0)
    def start():
        if with_direction:
            left = left_ref[...]
            total_ref[...] = jnp.dot(
                left, gram_ref[0], preferred_element_type=jnp.float32
            ) + jnp.dot(left, gram_ref[1], preferred_element_type=jnp.float32)
        else:
            total_ref[...] = jnp.zeros_like(total_ref)

    @pl.when(slot < count_ref[0])
    def add():
        factors = column_ref[:, block_ref[slot]].reshape(rows, rank)
        for at in range(0, rows, ROW_CHUNK):
            chunk = pl.ds(at, ROW_CHUNK)
            values = tiles_ref[0, chunk, :].astype(jnp.float32)
            if with_direction:
                scores = lax.dot_general(
                    left_ref[chunk, :],
                    factors,
                    (((1,), (1,)), ((), ())),
                    preferred_element_type=jnp.float32,
                )
                weighted = (values * scores).astype(jnp.bfloat16)
            else:
                weighted = (1.0 + values).astype(jnp.bfloat16)
            total_ref[chunk, :] += jnp.dot(weighted, factors, preferred_element_type=jnp.float32)

    @pl.when(slot == pl.num_programs(0) - 1)
    def finish():
        encode(total_ref, out_ref)


def encode(total_ref, out_ref):
    owners = out_ref.shape[0]
    share = total_ref.shape[0] // owners
    for owner in range(owners):
        block = total_ref[pl.ds(owner * share, share), :]
        largest = jnp.max(jnp.abs(block), axis=(0, 1), keepdims=True)
        level = jnp.ceil(jnp.log(jnp.maximum(largest, 1e-30)) * SCALE_STEPS)
        whole = jnp.round(block * (FULL_SCALE * jnp.exp(level * (-1.0 / SCALE_STEPS))))
        whole = whole.astype(jnp.int32).astype(jnp.int16)
        for at in range(0, block.shape[1], LANES):
            out_ref[owner, pl.ds(at // LANES * share, share), :] = whole[:, at : at + LANES]
        out_ref[owner, pl.ds(out_ref.shape[1] - SCALE_ROWS, SCALE_ROWS), :] = jnp.broadcast_to(
            level.astype(jnp.int32), (SCALE_ROWS, LANES)
        ).astype(jnp.int16)


def decode(parts, share, rank):
    levels = parts[:, -1:, :1].astype(jnp.float32)
    values = parts[:, : share * rank // LANES].astype(jnp.float32)
    total = jnp.sum(values * (jnp.exp(levels * (1.0 / SCALE_STEPS)) * (1.0 / FULL_SCALE)), axis=0)
    return jnp.concatenate([total[at : at + share] for at in range(0, total.shape[0], share)], axis=1)


def tile_sum(owners, count, blocks, tiles, column, left=None, gram=None):
    slots, rows, items = tiles.shape
    rank = column.shape[-1]
    whole = pl.BlockSpec(memory_space=pltpu.VMEM)
    scalar = pl.BlockSpec(memory_space=pltpu.SMEM)
    extra = () if left is None else (left, gram)
    return pl.pallas_call(
        functools.partial(tile_kernel, left is not None),
        grid=(slots,),
        out_shape=jax.ShapeDtypeStruct(
            (owners, rows // owners * rank // LANES + SCALE_ROWS, LANES), jnp.int16
        ),
        in_specs=[
            scalar,
            scalar,
            pl.BlockSpec((1, rows, items), lambda slot: (slot, 0, 0)),
            whole,
        ]
        + [whole] * len(extra),
        out_specs=whole,
        scratch_shapes=[pltpu.VMEM((rows, rank), jnp.float32)],
        compiler_params=pltpu.CompilerParams(vmem_limit_bytes=VMEM_BYTES),
    )(count, blocks, tiles, column, *extra)


def exchange(parts, axes):
    return lax.all_to_all(parts, axes, 0, 0, tiled=True)


def gather(block, axes):
    size = lax.axis_size(axes)
    return exchange(jnp.broadcast_to(block[None], (size,) + block.shape), axes)


def shards(confidence, tile_block, tile_count, item_factors):
    tiles = confidence[0, 0]
    blocks = tile_block[0, 0]
    count = tile_count[0]
    rows = tiles.shape[1]
    rank = item_factors.shape[1]

    column = gather(gather(item_factors, "z"), "x")
    flat = column.reshape(-1, rank)
    gram = lax.dot_general(
        flat, flat, (((0,), (0,)), ((), ())), preferred_element_type=jnp.float32
    )
    gram_high = gram.astype(jnp.bfloat16)
    gram_low = (gram - gram_high.astype(jnp.float32)).astype(jnp.bfloat16)
    gram = jnp.stack([gram_high, gram_low])

    owners = lax.axis_size(ITEMS)

    def reduce_rows(coded):
        return decode(exchange(coded, ITEMS), rows // owners, rank)

    right_side = reduce_rows(tile_sum(owners, count, blocks, tiles, column))
    solution = jnp.zeros_like(right_side)
    residual = right_side
    direction = right_side
    norm_now = jnp.sum(residual * residual, axis=1, keepdims=True)
    for step in range(STEPS):
        left = gather(direction.astype(jnp.bfloat16), ITEMS).reshape(rows, rank)
        image = (
            reduce_rows(tile_sum(owners, count, blocks, tiles, column, left, gram))
            + DAMPING * direction
        )
        step_size = norm_now / jnp.sum(direction * image, axis=1, keepdims=True)
        solution = solution + step_size * direction
        residual = residual - step_size * image
        norm_next = jnp.sum(residual * residual, axis=1, keepdims=True)
        direction = residual + norm_next / norm_now * direction
        norm_now = norm_next
    return (solution, residual)


def solution(mesh):
    chips = Mesh(mesh.devices.reshape(8, 8, 8, 2), USERS + ITEMS)
    in_specs = (
        P(USERS, ITEMS, None, None, None),
        P(USERS, ITEMS, None),
        P(USERS, ITEMS),
        P(ITEMS + USERS, None),
    )
    out_specs = (P(USERS + ITEMS, None), P(USERS + ITEMS, None))
    return jax.shard_map(shards, mesh=chips, in_specs=in_specs, out_specs=out_specs, check_vma=False)
```

```python
import functools

import jax
import jax.numpy as jnp
from jax import lax
from jax.experimental import pallas as pl
from jax.experimental.pallas import tpu as pltpu
from jax.sharding import Mesh
from jax.sharding import PartitionSpec as P

STEPS = 2
DAMPING = 0.1
ROW_CHUNK = 256
VMEM_BYTES = 24 * 1024 * 1024
LANES = 128
SCALE_ROWS = 8
SCALE_STEPS = 64.0
FULL_SCALE = 32000.0
USERS = ("z", "x")
ITEMS = ("y", "core")
WHOLE = pl.BlockSpec(memory_space=pltpu.VMEM)
SCALARS = pl.BlockSpec(memory_space=pltpu.SMEM)
FAR = pl.BlockSpec(memory_space=pltpu.HBM)


def spread_kernel(first_ref, factors_ref, out_ref):
    piece = factors_ref.shape[0]
    share = out_ref.shape[1] - piece
    gram = jnp.sum(first_ref[:, pl.ds(0, share), :].astype(jnp.float32), axis=0)
    gram = gram.astype(jnp.bfloat16)
    for peer in range(out_ref.shape[0]):
        out_ref[peer, pl.ds(0, piece), :] = factors_ref[...]
        out_ref[peer, pl.ds(piece, share), :] = gram


def spread(first, factors, peers, share):
    piece, rank = factors.shape
    return pl.pallas_call(
        spread_kernel,
        out_shape=jax.ShapeDtypeStruct((peers, piece + share, rank), factors.dtype),
        in_specs=[WHOLE, WHOLE],
        out_specs=WHOLE,
        compiler_params=pltpu.CompilerParams(vmem_limit_bytes=VMEM_BYTES),
    )(first, factors)


def pick_kernel(wanted_ref, pieces_ref, out_ref):
    peers, height, rank = out_ref.shape
    share = rank // peers
    piece = pieces_ref.shape[1] - share
    slots = (height - share) // piece
    gram = jnp.sum(pieces_ref[:, pl.ds(piece, share), :].astype(jnp.float32), axis=0)
    gram = gram.astype(jnp.bfloat16)
    for peer in range(peers):
        for slot in range(slots):
            out_ref[peer, pl.ds(slot * piece, piece), :] = pieces_ref[
                wanted_ref[peer, slot], pl.ds(0, piece), :
            ]
        out_ref[peer, pl.ds(slots * piece, share), :] = gram


def pick(wanted, pieces, slots):
    peers = wanted.shape[0]
    _, height, rank = pieces.shape
    share = rank // peers
    return pl.pallas_call(
        pick_kernel,
        out_shape=jax.ShapeDtypeStruct(
            (peers, slots * (height - share) + share, rank), pieces.dtype
        ),
        in_specs=[SCALARS, WHOLE],
        out_specs=WHOLE,
        compiler_params=pltpu.CompilerParams(vmem_limit_bytes=VMEM_BYTES),
    )(wanted, pieces)


def tile_kernel(with_direction, count_ref, tiles_ref, factors_ref, *refs):
    if with_direction:
        left_ref, out_ref, total_ref, held_ref, arrived = refs
    else:
        out_ref, total_ref, held_ref, arrived = refs
    slots = held_ref.shape[0]
    rows, rank = total_ref.shape
    piece = rows // factors_ref.shape[0]
    step = min(ROW_CHUNK, rows)

    def fetch(slot):
        return pltpu.make_async_copy(tiles_ref.at[slot], held_ref.at[slot], arrived.at[slot])

    for slot in range(slots):

        @pl.when(slot < count_ref[0])
        def ask():
            fetch(slot).start()

    if with_direction:
        share = factors_ref.shape[1] - slots * piece
        gram = factors_ref[:, pl.ds(slots * piece, share), :].reshape(rank, rank)
        total_ref[...] = jnp.dot(left_ref[...], gram, preferred_element_type=jnp.float32)
    else:
        total_ref[...] = jnp.zeros_like(total_ref)

    for slot in range(slots):

        @pl.when(slot < count_ref[0])
        def add():
            factors = factors_ref[:, pl.ds(slot * piece, piece), :].reshape(rows, rank)
            fetch(slot).wait()
            for at in range(0, rows, step):
                chunk = pl.ds(at, step)
                values = held_ref[slot, chunk, :].astype(jnp.float32)
                if with_direction:
                    scores = lax.dot_general(
                        left_ref[chunk, :],
                        factors,
                        (((1,), (1,)), ((), ())),
                        preferred_element_type=jnp.float32,
                    )
                    weighted = (values * scores).astype(jnp.bfloat16)
                else:
                    weighted = (1.0 + values).astype(jnp.bfloat16)
                total_ref[chunk, :] += jnp.dot(
                    weighted, factors, preferred_element_type=jnp.float32
                )

    encode(total_ref, out_ref)


def encode(total_ref, out_ref):
    owners = out_ref.shape[0]
    share = total_ref.shape[0] // owners
    for owner in range(owners):
        block = total_ref[pl.ds(owner * share, share), :]
        largest = jnp.max(jnp.abs(block), axis=(0, 1), keepdims=True)
        level = jnp.ceil(jnp.log(jnp.maximum(largest, 1e-30)) * SCALE_STEPS)
        whole = jnp.round(block * (FULL_SCALE * jnp.exp(level * (-1.0 / SCALE_STEPS))))
        whole = whole.astype(jnp.int32).astype(jnp.int16)
        for at in range(0, block.shape[1], LANES):
            out_ref[owner, pl.ds(at // LANES * share, share), :] = whole[:, at : at + LANES]
        out_ref[owner, pl.ds(out_ref.shape[1] - SCALE_ROWS, SCALE_ROWS), :] = jnp.broadcast_to(
            level.astype(jnp.int32), (SCALE_ROWS, LANES)
        ).astype(jnp.int16)


def decode(parts, share, rank):
    levels = parts[:, -1:, :1].astype(jnp.float32)
    values = parts[:, : share * rank // LANES].astype(jnp.float32)
    total = jnp.sum(values * (jnp.exp(levels * (1.0 / SCALE_STEPS)) * (1.0 / FULL_SCALE)), axis=0)
    return jnp.concatenate([total[at : at + share] for at in range(0, total.shape[0], share)], axis=1)


def tile_sum(owners, count, tiles, factors, left=None):
    slots, rows, items = tiles.shape
    rank = factors.shape[-1]
    extra = () if left is None else (left,)
    return pl.pallas_call(
        functools.partial(tile_kernel, left is not None),
        out_shape=jax.ShapeDtypeStruct(
            (owners, rows // owners * rank // LANES + SCALE_ROWS, LANES), jnp.int16
        ),
        in_specs=[SCALARS, FAR, WHOLE] + [WHOLE] * len(extra),
        out_specs=WHOLE,
        scratch_shapes=[
            pltpu.VMEM((rows, rank), jnp.float32),
            pltpu.VMEM((slots, rows, items), jnp.bfloat16),
            pltpu.SemaphoreType.DMA((slots,)),
        ],
        compiler_params=pltpu.CompilerParams(vmem_limit_bytes=VMEM_BYTES),
    )(count, tiles, factors, *extra)


def exchange(parts, axes):
    return lax.all_to_all(parts, axes, 0, 0, tiled=True)


def gather(block, axes):
    size = lax.axis_size(axes)
    return exchange(jnp.broadcast_to(block[None], (size,) + block.shape), axes)


def shards(confidence, tile_block, tile_count, item_factors):
    tiles = confidence[0, 0]
    blocks = tile_block[0, 0]
    count = tile_count[0]
    slots, rows, _ = tiles.shape
    rank = item_factors.shape[1]
    owners = lax.axis_size(ITEMS)

    peers = lax.axis_size("x")
    share = rank // peers
    local = lax.dot_general(
        item_factors, item_factors, (((0,), (0,)), ((), ())), preferred_element_type=jnp.float32
    ).astype(jnp.bfloat16)
    named = jnp.pad(blocks.astype(jnp.bfloat16), (0, rank - slots))
    first = jnp.concatenate(
        [local.reshape(peers, share, rank), jnp.broadcast_to(named, (peers, 8, rank))], axis=1
    )
    first = exchange(first, "x")
    wanted = first[:, share, :LANES].astype(jnp.int32)
    pieces = exchange(spread(first, item_factors, lax.axis_size("z"), share), "z")
    factors = exchange(pick(wanted, pieces, slots), "x")

    def reduce_rows(coded):
        return decode(exchange(coded, ITEMS), rows // owners, rank)

    right_side = reduce_rows(tile_sum(owners, count, tiles, factors))
    solution = jnp.zeros_like(right_side)
    residual = right_side
    direction = right_side
    norm_now = jnp.sum(residual * residual, axis=1, keepdims=True)
    for step in range(STEPS):
        left = gather(direction.astype(jnp.bfloat16), ITEMS).reshape(rows, rank)
        image = (
            reduce_rows(tile_sum(owners, count, tiles, factors, left))
            + DAMPING * direction
        )
        step_size = norm_now / jnp.sum(direction * image, axis=1, keepdims=True)
        solution = solution + step_size * direction
        residual = residual - step_size * image
        norm_next = jnp.sum(residual * residual, axis=1, keepdims=True)
        direction = residual + norm_next / norm_now * direction
        norm_now = norm_next
    return (solution, residual)


def solution(mesh):
    chips = Mesh(mesh.devices.reshape(8, 8, 8, 2), USERS + ITEMS)
    in_specs = (
        P(USERS, ITEMS, None, None, None),
        P(USERS, ITEMS, None),
        P(USERS, ITEMS),
        P(ITEMS + USERS, None),
    )
    out_specs = (P(USERS + ITEMS, None), P(USERS + ITEMS, None))
    return jax.shard_map(shards, mesh=chips, in_specs=in_specs, out_specs=out_specs, check_vma=False)
```

```python
import functools

import jax
import jax.numpy as jnp
from jax import lax
from jax.experimental import pallas as pl
from jax.experimental.pallas import tpu as pltpu
from jax.sharding import Mesh
from jax.sharding import PartitionSpec as P

STEPS = 2
DAMPING = 0.1
ROW_CHUNK = 256
VMEM_BYTES = 24 * 1024 * 1024
LANES = 128
SCALE_ROWS = 8
NAME_ROWS = 8
SCALE_STEPS = 64.0
FULL_SCALE = 32000.0
USERS = ("z", "x")
ITEMS = ("y", "core")
WHOLE = pl.BlockSpec(memory_space=pltpu.VMEM)
SCALARS = pl.BlockSpec(memory_space=pltpu.SMEM)
FAR = pl.BlockSpec(memory_space=pltpu.HBM)


def first_kernel(blocks_ref, pieces_ref, out_ref):
    peers, height, rank = out_ref.shape
    share = rank // peers
    slots = blocks_ref.shape[2]
    flat = pieces_ref[...].reshape(-1, rank)
    gram = lax.dot_general(
        flat, flat, (((0,), (0,)), ((), ())), preferred_element_type=jnp.float32
    ).astype(jnp.bfloat16)
    lane = lax.broadcasted_iota(jnp.int32, (height - share, rank), 1)
    named = jnp.zeros((height - share, rank), jnp.float32)
    for slot in range(slots):
        named = jnp.where(lane == slot, blocks_ref[0, 0, slot].astype(jnp.float32), named)
    for peer in range(peers):
        out_ref[peer, pl.ds(0, share), :] = gram[peer * share : (peer + 1) * share]
        out_ref[peer, pl.ds(share, height - share), :] = named.astype(jnp.bfloat16)


def first(tile_block, pieces, peers):
    rank = pieces.shape[-1]
    return pl.pallas_call(
        first_kernel,
        out_shape=jax.ShapeDtypeStruct((peers, rank // peers + NAME_ROWS, rank), pieces.dtype),
        in_specs=[SCALARS, WHOLE],
        out_specs=WHOLE,
        compiler_params=pltpu.CompilerParams(vmem_limit_bytes=VMEM_BYTES),
    )(tile_block, pieces)


def pick_kernel(wanted_ref, pieces_ref, grams_ref, out_ref):
    peers, height, rank = out_ref.shape
    share = rank // peers
    piece = pieces_ref.shape[1]
    slots = (height - share) // piece
    gram = jnp.sum(grams_ref[:, pl.ds(0, share), :].astype(jnp.float32), axis=0)
    gram = gram.astype(jnp.bfloat16)
    for peer in range(peers):
        for slot in range(slots):
            out_ref[peer, pl.ds(slot * piece, piece), :] = pieces_ref[wanted_ref[peer, slot]]
        out_ref[peer, pl.ds(slots * piece, share), :] = gram


def pick(wanted, pieces, grams, slots):
    peers = wanted.shape[0]
    _, piece, rank = pieces.shape
    return pl.pallas_call(
        pick_kernel,
        out_shape=jax.ShapeDtypeStruct((peers, slots * piece + rank // peers, rank), pieces.dtype),
        in_specs=[SCALARS, WHOLE, WHOLE],
        out_specs=WHOLE,
        compiler_params=pltpu.CompilerParams(vmem_limit_bytes=VMEM_BYTES),
    )(wanted, pieces, grams)


def hold_kernel(tiles_ref, held_ref, arrived):
    copy = pltpu.make_async_copy(tiles_ref, held_ref, arrived)
    copy.start()
    copy.wait()


def hold(tiles):
    return pl.pallas_call(
        hold_kernel,
        out_shape=jax.ShapeDtypeStruct(tiles.shape, tiles.dtype),
        in_specs=[FAR],
        out_specs=WHOLE,
        scratch_shapes=[pltpu.SemaphoreType.DMA],
        compiler_params=pltpu.CompilerParams(vmem_limit_bytes=VMEM_BYTES),
        cost_estimate=pl.CostEstimate(flops=0, transcendentals=0, bytes_accessed=4 * tiles.size),
    )(tiles)


def tile_kernel(with_direction, count_ref, tiles_ref, factors_ref, *refs):
    if with_direction:
        left_ref, out_ref, total_ref = refs
    else:
        out_ref, total_ref = refs
    slots = tiles_ref.shape[0]
    rows, rank = total_ref.shape
    piece = rows // factors_ref.shape[0]
    step = min(ROW_CHUNK, rows)

    if with_direction:
        share = factors_ref.shape[1] - slots * piece
        gram = factors_ref[:, pl.ds(slots * piece, share), :].reshape(rank, rank)
        total_ref[...] = jnp.dot(left_ref[...], gram, preferred_element_type=jnp.float32)
    else:
        total_ref[...] = jnp.zeros_like(total_ref)

    for slot in range(slots):

        @pl.when(slot < count_ref[0, 0])
        def add():
            factors = factors_ref[:, pl.ds(slot * piece, piece), :].reshape(rows, rank)
            for at in range(0, rows, step):
                chunk = pl.ds(at, step)
                values = tiles_ref[slot, chunk, :].astype(jnp.float32)
                if with_direction:
                    scores = lax.dot_general(
                        left_ref[chunk, :],
                        factors,
                        (((1,), (1,)), ((), ())),
                        preferred_element_type=jnp.float32,
                    )
                    weighted = (values * scores).astype(jnp.bfloat16)
                else:
                    weighted = (1.0 + values).astype(jnp.bfloat16)
                total_ref[chunk, :] += jnp.dot(
                    weighted, factors, preferred_element_type=jnp.float32
                )

    encode(total_ref, out_ref)


def encode(total_ref, out_ref):
    owners = out_ref.shape[0]
    share = total_ref.shape[0] // owners
    for owner in range(owners):
        block = total_ref[pl.ds(owner * share, share), :]
        largest = jnp.max(jnp.abs(block), axis=(0, 1), keepdims=True)
        level = jnp.ceil(jnp.log(jnp.maximum(largest, 1e-30)) * SCALE_STEPS)
        whole = jnp.round(block * (FULL_SCALE * jnp.exp(level * (-1.0 / SCALE_STEPS))))
        whole = whole.astype(jnp.int32).astype(jnp.int16)
        for at in range(0, block.shape[1], LANES):
            out_ref[owner, pl.ds(at // LANES * share, share), :] = whole[:, at : at + LANES]
        out_ref[owner, pl.ds(out_ref.shape[1] - SCALE_ROWS, SCALE_ROWS), :] = jnp.broadcast_to(
            level.astype(jnp.int32), (SCALE_ROWS, LANES)
        ).astype(jnp.int16)


def decode(parts, share, rank):
    levels = parts[:, -1:, :1].astype(jnp.float32)
    values = parts[:, : share * rank // LANES].astype(jnp.float32)
    total = jnp.sum(values * (jnp.exp(levels * (1.0 / SCALE_STEPS)) * (1.0 / FULL_SCALE)), axis=0)
    return jnp.concatenate([total[at : at + share] for at in range(0, total.shape[0], share)], axis=1)


def tile_sum(owners, tile_count, tiles, factors, left=None):
    slots, rows, items = tiles.shape
    rank = factors.shape[-1]
    extra = () if left is None else (left,)
    return pl.pallas_call(
        functools.partial(tile_kernel, left is not None),
        out_shape=jax.ShapeDtypeStruct(
            (owners, rows // owners * rank // LANES + SCALE_ROWS, LANES), jnp.int16
        ),
        in_specs=[SCALARS, WHOLE, WHOLE] + [WHOLE] * len(extra),
        out_specs=WHOLE,
        scratch_shapes=[
            pltpu.VMEM((rows, rank), jnp.float32),
        ],
        compiler_params=pltpu.CompilerParams(vmem_limit_bytes=VMEM_BYTES),
    )(tile_count, tiles, factors, *extra)


def exchange(parts, axes):
    return lax.all_to_all(parts, axes, 0, 0, tiled=True)


def gather(block, axes):
    size = lax.axis_size(axes)
    return exchange(jnp.broadcast_to(block[None], (size,) + block.shape), axes)


def shards(confidence, tile_block, tile_count, item_factors):
    tiles = hold(confidence[0, 0])
    slots, rows, _ = tiles.shape
    rank = item_factors.shape[1]
    owners = lax.axis_size(ITEMS)

    peers = lax.axis_size("x")
    share = rank // peers
    pieces = gather(item_factors, "z")
    grams = exchange(first(tile_block, pieces, peers), "x")
    wanted = grams[:, share, :LANES].astype(jnp.int32)
    factors = exchange(pick(wanted, pieces, grams, slots), "x")

    def reduce_rows(coded):
        return decode(exchange(coded, ITEMS), rows // owners, rank)

    right_side = reduce_rows(tile_sum(owners, tile_count, tiles, factors))
    solution = jnp.zeros_like(right_side)
    residual = right_side
    direction = right_side
    norm_now = jnp.sum(residual * residual, axis=1, keepdims=True)
    for step in range(STEPS):
        left = gather(direction.astype(jnp.bfloat16), ITEMS).reshape(rows, rank)
        image = (
            reduce_rows(tile_sum(owners, tile_count, tiles, factors, left))
            + DAMPING * direction
        )
        step_size = norm_now / jnp.sum(direction * image, axis=1, keepdims=True)
        solution = solution + step_size * direction
        residual = residual - step_size * image
        norm_next = jnp.sum(residual * residual, axis=1, keepdims=True)
        direction = residual + norm_next / norm_now * direction
        norm_now = norm_next
    return (solution, residual)


def solution(mesh):
    chips = Mesh(mesh.devices.reshape(8, 8, 8, 2), USERS + ITEMS)
    in_specs = (
        P(USERS, ITEMS, None, None, None),
        P(USERS, ITEMS, None),
        P(USERS, ITEMS),
        P(ITEMS + USERS, None),
    )
    out_specs = (P(USERS + ITEMS, None), P(USERS + ITEMS, None))
    return jax.shard_map(shards, mesh=chips, in_specs=in_specs, out_specs=out_specs, check_vma=False)
```

```python
import functools

import jax
import jax.numpy as jnp
from jax import lax
from jax.experimental import pallas as pl
from jax.experimental.pallas import tpu as pltpu
from jax.sharding import Mesh
from jax.sharding import PartitionSpec as P

STEPS = 2
DAMPING = 0.1
ROW_CHUNK = 256
VMEM_BYTES = 24 * 1024 * 1024
LANES = 128
SCALE_ROWS = 8
NAME_ROWS = 8
SCALE_STEPS = 64.0
FULL_SCALE = 32000.0
USERS = ("z", "x")
ITEMS = ("y", "core")
WHOLE = pl.BlockSpec(memory_space=pltpu.VMEM)
SCALARS = pl.BlockSpec(memory_space=pltpu.SMEM)
FAR = pl.BlockSpec(memory_space=pltpu.HBM)


def first_kernel(names_ref, pieces_ref, out_ref):
    peers, height, rank = out_ref.shape
    share = rank // peers
    flat = pieces_ref[...].reshape(-1, rank)
    gram = lax.dot_general(
        flat, flat, (((0,), (0,)), ((), ())), preferred_element_type=jnp.float32
    ).astype(jnp.bfloat16)
    names = names_ref[...]
    for peer in range(peers):
        out_ref[peer, pl.ds(0, share), :] = gram[peer * share : (peer + 1) * share]
        out_ref[peer, pl.ds(share, height - share), :] = names


def first(names, pieces, peers):
    rank = pieces.shape[-1]
    return pl.pallas_call(
        first_kernel,
        out_shape=jax.ShapeDtypeStruct((peers, rank // peers + NAME_ROWS, rank), pieces.dtype),
        in_specs=[WHOLE, WHOLE],
        out_specs=WHOLE,
        compiler_params=pltpu.CompilerParams(vmem_limit_bytes=VMEM_BYTES),
    )(names, pieces)


def pick_kernel(wanted_ref, pieces_ref, grams_ref, out_ref):
    peers, height, rank = out_ref.shape
    share = rank // peers
    blocks, piece, _ = pieces_ref.shape
    slots = (height - share) // piece
    gram = jnp.sum(grams_ref[:, pl.ds(0, share), :].astype(jnp.float32), axis=0)
    gram = gram.astype(jnp.bfloat16)
    for peer in range(peers):
        for slot in range(slots):
            name = wanted_ref[peer, slot]
            rows = pl.ds(slot * piece, piece)

            @pl.when(name < blocks)
            def live():
                out_ref[peer, rows, :] = pieces_ref[name]

            @pl.when(name >= blocks)
            def dead():
                out_ref[peer, rows, :] = jnp.zeros((piece, rank), out_ref.dtype)

        out_ref[peer, pl.ds(slots * piece, share), :] = gram


def pick(wanted, pieces, grams, slots):
    peers = wanted.shape[0]
    _, piece, rank = pieces.shape
    return pl.pallas_call(
        pick_kernel,
        out_shape=jax.ShapeDtypeStruct((peers, slots * piece + rank // peers, rank), pieces.dtype),
        in_specs=[SCALARS, WHOLE, WHOLE],
        out_specs=WHOLE,
        compiler_params=pltpu.CompilerParams(vmem_limit_bytes=VMEM_BYTES),
    )(wanted, pieces, grams)


def hold_kernel(tiles_ref, held_ref, arrived):
    copy = pltpu.make_async_copy(tiles_ref, held_ref, arrived)
    copy.start()
    copy.wait()


def hold(tiles):
    return pl.pallas_call(
        hold_kernel,
        out_shape=jax.ShapeDtypeStruct(tiles.shape, tiles.dtype),
        in_specs=[FAR],
        out_specs=WHOLE,
        scratch_shapes=[pltpu.SemaphoreType.DMA],
        compiler_params=pltpu.CompilerParams(vmem_limit_bytes=VMEM_BYTES),
        cost_estimate=pl.CostEstimate(flops=0, transcendentals=0, bytes_accessed=4 * tiles.size),
    )(tiles)


def tile_kernel(with_direction, tiles_ref, factors_ref, *refs):
    if with_direction:
        left_ref, out_ref, total_ref = refs
    else:
        out_ref, total_ref = refs
    slots = tiles_ref.shape[0]
    rows, rank = total_ref.shape
    piece = rows // factors_ref.shape[0]
    step = min(ROW_CHUNK, rows)
    if with_direction:
        share = factors_ref.shape[1] - slots * piece
        gram = factors_ref[:, pl.ds(slots * piece, share), :].reshape(rank, rank)
    for at in range(0, rows, step):
        chunk = pl.ds(at, step)
        if with_direction:
            left = left_ref[chunk, :]
            total = jnp.dot(left, gram, preferred_element_type=jnp.float32)
        else:
            total = jnp.zeros((step, rank), jnp.float32)
        for slot in range(slots):
            factors = factors_ref[:, pl.ds(slot * piece, piece), :].reshape(rows, rank)
            values = tiles_ref[slot, chunk, :].astype(jnp.float32)
            if with_direction:
                scores = lax.dot_general(
                    left, factors, (((1,), (1,)), ((), ())), preferred_element_type=jnp.float32
                )
                weighted = (values * scores).astype(jnp.bfloat16)
            else:
                weighted = (1.0 + values).astype(jnp.bfloat16)
            total += jnp.dot(weighted, factors, preferred_element_type=jnp.float32)
        total_ref[chunk, :] = total
    encode(total_ref, out_ref)


def encode(total_ref, out_ref):
    owners = out_ref.shape[0]
    share = total_ref.shape[0] // owners
    for owner in range(owners):
        block = total_ref[pl.ds(owner * share, share), :]
        largest = jnp.max(jnp.abs(block), axis=(0, 1), keepdims=True)
        level = jnp.ceil(jnp.log(jnp.maximum(largest, 1e-30)) * SCALE_STEPS)
        whole = jnp.round(block * (FULL_SCALE * jnp.exp(level * (-1.0 / SCALE_STEPS))))
        whole = whole.astype(jnp.int32).astype(jnp.int16)
        for at in range(0, block.shape[1], LANES):
            out_ref[owner, pl.ds(at // LANES * share, share), :] = whole[:, at : at + LANES]
        out_ref[owner, pl.ds(out_ref.shape[1] - SCALE_ROWS, SCALE_ROWS), :] = jnp.broadcast_to(
            level.astype(jnp.int32), (SCALE_ROWS, LANES)
        ).astype(jnp.int16)


def decode(parts, share, rank):
    levels = parts[:, -1:, :1].astype(jnp.float32)
    values = parts[:, : share * rank // LANES].astype(jnp.float32)
    total = jnp.sum(values * (jnp.exp(levels * (1.0 / SCALE_STEPS)) * (1.0 / FULL_SCALE)), axis=0)
    return jnp.concatenate([total[at : at + share] for at in range(0, total.shape[0], share)], axis=1)


def tile_sum(owners, tiles, factors, left=None):
    slots, rows, items = tiles.shape
    rank = factors.shape[-1]
    extra = () if left is None else (left,)
    return pl.pallas_call(
        functools.partial(tile_kernel, left is not None),
        out_shape=jax.ShapeDtypeStruct(
            (owners, rows // owners * rank // LANES + SCALE_ROWS, LANES), jnp.int16
        ),
        in_specs=[WHOLE, WHOLE] + [WHOLE] * len(extra),
        out_specs=WHOLE,
        scratch_shapes=[
            pltpu.VMEM((rows, rank), jnp.float32),
        ],
        compiler_params=pltpu.CompilerParams(vmem_limit_bytes=VMEM_BYTES),
    )(tiles, factors, *extra)


def exchange(parts, axes):
    return lax.all_to_all(parts, axes, 0, 0, tiled=True)


def gather(block, axes):
    size = lax.axis_size(axes)
    return exchange(jnp.broadcast_to(block[None], (size,) + block.shape), axes)


def shards(confidence, tile_block, tile_count, item_factors):
    tiles = hold(confidence[0, 0])
    slots, rows, _ = tiles.shape
    rank = item_factors.shape[1]
    owners = lax.axis_size(ITEMS)

    peers = lax.axis_size("x")
    share = rank // peers
    pieces = gather(item_factors, "z")
    live = jnp.arange(slots, dtype=jnp.int32)[None] < tile_count
    names = jnp.where(live, tile_block[0], lax.axis_size("z")).astype(jnp.bfloat16)
    names = jnp.pad(names, ((0, 0), (0, rank - slots)))
    names = jnp.broadcast_to(names, (NAME_ROWS, rank))
    grams = exchange(first(names, pieces, peers), "x")
    wanted = grams[:, share, :LANES].astype(jnp.int32)
    factors = exchange(pick(wanted, pieces, grams, slots), "x")

    def reduce_rows(coded):
        return decode(exchange(coded, ITEMS), rows // owners, rank)

    right_side = reduce_rows(tile_sum(owners, tiles, factors))
    solution = jnp.zeros_like(right_side)
    residual = right_side
    direction = right_side
    norm_now = jnp.sum(residual * residual, axis=1, keepdims=True)
    for step in range(STEPS):
        left = gather(direction.astype(jnp.bfloat16), ITEMS).reshape(rows, rank)
        image = (
            reduce_rows(tile_sum(owners, tiles, factors, left))
            + DAMPING * direction
        )
        step_size = norm_now / jnp.sum(direction * image, axis=1, keepdims=True)
        solution = solution + step_size * direction
        residual = residual - step_size * image
        norm_next = jnp.sum(residual * residual, axis=1, keepdims=True)
        direction = residual + norm_next / norm_now * direction
        norm_now = norm_next
    return (solution, residual)


def solution(mesh):
    chips = Mesh(mesh.devices.reshape(8, 8, 8, 2), USERS + ITEMS)
    in_specs = (
        P(USERS, ITEMS, None, None, None),
        P(USERS, ITEMS, None),
        P(USERS, ITEMS),
        P(ITEMS + USERS, None),
    )
    out_specs = (P(USERS + ITEMS, None), P(USERS + ITEMS, None))
    return jax.shard_map(shards, mesh=chips, in_specs=in_specs, out_specs=out_specs, check_vma=False)
```

```python
import functools

import jax
import jax.numpy as jnp
from jax import lax
from jax.experimental import pallas as pl
from jax.experimental.pallas import tpu as pltpu
from jax.sharding import Mesh
from jax.sharding import PartitionSpec as P

STEPS = 2
DAMPING = 0.1
ROW_CHUNK = 256
VMEM_BYTES = 24 * 1024 * 1024
LANES = 128
SCALE_ROWS = 16
NAME_ROWS = 16
SCALE_STEPS = 64.0
FULL_SCALE = 32000.0
USERS = ("z", "x")
ITEMS = ("y", "core")
WHOLE = pl.BlockSpec(memory_space=pltpu.VMEM)
SCALARS = pl.BlockSpec(memory_space=pltpu.SMEM)
FAR = pl.BlockSpec(memory_space=pltpu.HBM)


def first_kernel(names_ref, pieces_ref, out_ref):
    peers = out_ref.shape[0]
    rank = pieces_ref.shape[2]
    share = rank // peers
    strips = rank // LANES
    flat = pieces_ref[...].reshape(-1, rank)
    gram = lax.dot_general(
        flat, flat, (((0,), (0,)), ((), ())), preferred_element_type=jnp.float32
    ).astype(jnp.bfloat16)
    names = names_ref[...]
    for peer in range(peers):
        rows = gram[peer * share : (peer + 1) * share]
        for strip in range(strips):
            out_ref[peer, pl.ds(strip * share, share), :] = rows[
                :, strip * LANES : (strip + 1) * LANES
            ]
        out_ref[peer, pl.ds(strips * share, NAME_ROWS), :] = names


def first(names, pieces, peers):
    rank = pieces.shape[-1]
    return pl.pallas_call(
        first_kernel,
        out_shape=jax.ShapeDtypeStruct(
            (peers, rank // peers * rank // LANES + NAME_ROWS, LANES), pieces.dtype
        ),
        in_specs=[WHOLE, WHOLE],
        out_specs=WHOLE,
        compiler_params=pltpu.CompilerParams(vmem_limit_bytes=VMEM_BYTES),
    )(names, pieces)


def pick_kernel(wanted_ref, pieces_ref, grams_ref, out_ref):
    peers, height, rank = out_ref.shape
    share = rank // peers
    blocks, piece, _ = pieces_ref.shape
    slots = (height - share) // piece
    gram = jnp.concatenate(
        [
            jnp.sum(grams_ref[:, pl.ds(strip * share, share), :].astype(jnp.float32), axis=0)
            for strip in range(rank // LANES)
        ],
        axis=1,
    ).astype(jnp.bfloat16)
    for peer in range(peers):
        for slot in range(slots):
            name = wanted_ref[peer, slot]
            rows = pl.ds(slot * piece, piece)

            @pl.when(name < blocks)
            def live():
                out_ref[peer, rows, :] = pieces_ref[name]

            @pl.when(name >= blocks)
            def dead():
                out_ref[peer, rows, :] = jnp.zeros((piece, rank), out_ref.dtype)

        out_ref[peer, pl.ds(slots * piece, share), :] = gram


def pick(wanted, pieces, grams, slots):
    peers = wanted.shape[0]
    _, piece, rank = pieces.shape
    return pl.pallas_call(
        pick_kernel,
        out_shape=jax.ShapeDtypeStruct((peers, slots * piece + rank // peers, rank), pieces.dtype),
        in_specs=[SCALARS, WHOLE, WHOLE],
        out_specs=WHOLE,
        compiler_params=pltpu.CompilerParams(vmem_limit_bytes=VMEM_BYTES),
    )(wanted, pieces, grams)


def hold_kernel(tiles_ref, held_ref, arrived):
    copy = pltpu.make_async_copy(tiles_ref, held_ref, arrived)
    copy.start()
    copy.wait()


def hold(tiles):
    return pl.pallas_call(
        hold_kernel,
        out_shape=jax.ShapeDtypeStruct(tiles.shape, tiles.dtype),
        in_specs=[FAR],
        out_specs=WHOLE,
        scratch_shapes=[pltpu.SemaphoreType.DMA],
        compiler_params=pltpu.CompilerParams(vmem_limit_bytes=VMEM_BYTES),
        cost_estimate=pl.CostEstimate(flops=0, transcendentals=0, bytes_accessed=4 * tiles.size),
    )(tiles)


def tile_kernel(with_direction, tiles_ref, factors_ref, *refs):
    if with_direction:
        left_ref, out_ref, total_ref = refs
    else:
        out_ref, total_ref = refs
    slots = tiles_ref.shape[0]
    rows, rank = total_ref.shape
    piece = rows // factors_ref.shape[0]
    step = min(ROW_CHUNK, rows)
    if with_direction:
        share = factors_ref.shape[1] - slots * piece
        gram = factors_ref[:, pl.ds(slots * piece, share), :].reshape(rank, rank)
    for at in range(0, rows, step):
        chunk = pl.ds(at, step)
        if with_direction:
            left = left_ref[chunk, :]
            total = jnp.dot(left, gram, preferred_element_type=jnp.float32)
        else:
            total = jnp.zeros((step, rank), jnp.float32)
        for slot in range(slots):
            factors = factors_ref[:, pl.ds(slot * piece, piece), :].reshape(rows, rank)
            values = tiles_ref[slot, chunk, :].astype(jnp.float32)
            if with_direction:
                scores = lax.dot_general(
                    left, factors, (((1,), (1,)), ((), ())), preferred_element_type=jnp.float32
                )
                weighted = (values * scores).astype(jnp.bfloat16)
            else:
                weighted = (1.0 + values).astype(jnp.bfloat16)
            total += jnp.dot(weighted, factors, preferred_element_type=jnp.float32)
        total_ref[chunk, :] = total
    encode(total_ref, out_ref)


def encode(total_ref, out_ref):
    owners = out_ref.shape[0]
    share = total_ref.shape[0] // owners
    for owner in range(owners):
        block = total_ref[pl.ds(owner * share, share), :]
        largest = jnp.max(jnp.abs(block), axis=(0, 1), keepdims=True)
        level = jnp.ceil(jnp.log(jnp.maximum(largest, 1e-30)) * SCALE_STEPS)
        whole = jnp.round(block * (FULL_SCALE * jnp.exp(level * (-1.0 / SCALE_STEPS))))
        whole = whole.astype(jnp.int32).astype(jnp.int16)
        for at in range(0, block.shape[1], LANES):
            out_ref[owner, pl.ds(at // LANES * share, share), :] = whole[:, at : at + LANES]
        out_ref[owner, pl.ds(out_ref.shape[1] - SCALE_ROWS, SCALE_ROWS), :] = jnp.broadcast_to(
            level.astype(jnp.int32), (SCALE_ROWS, LANES)
        ).astype(jnp.int16)


def decode(parts, share, rank):
    levels = parts[:, -1:, :1].astype(jnp.float32)
    values = parts[:, : share * rank // LANES].astype(jnp.float32)
    total = jnp.sum(values * (jnp.exp(levels * (1.0 / SCALE_STEPS)) * (1.0 / FULL_SCALE)), axis=0)
    return jnp.concatenate([total[at : at + share] for at in range(0, total.shape[0], share)], axis=1)


def tile_sum(owners, tiles, factors, left=None):
    slots, rows, items = tiles.shape
    rank = factors.shape[-1]
    extra = () if left is None else (left,)
    return pl.pallas_call(
        functools.partial(tile_kernel, left is not None),
        out_shape=jax.ShapeDtypeStruct(
            (owners, rows // owners * rank // LANES + SCALE_ROWS, LANES), jnp.int16
        ),
        in_specs=[WHOLE, WHOLE] + [WHOLE] * len(extra),
        out_specs=WHOLE,
        scratch_shapes=[
            pltpu.VMEM((rows, rank), jnp.float32),
        ],
        compiler_params=pltpu.CompilerParams(vmem_limit_bytes=VMEM_BYTES),
    )(tiles, factors, *extra)


def exchange(parts, axes):
    return lax.all_to_all(parts, axes, 0, 0, tiled=True)


def gather(block, axes):
    size = lax.axis_size(axes)
    return exchange(jnp.broadcast_to(block[None], (size,) + block.shape), axes)


def shards(confidence, tile_block, tile_count, item_factors):
    tiles = hold(confidence[0, 0])
    slots, rows, _ = tiles.shape
    rank = item_factors.shape[1]
    owners = lax.axis_size(ITEMS)

    peers = lax.axis_size("x")
    pieces = gather(item_factors, "z")
    live = jnp.arange(slots, dtype=jnp.int32)[None] < tile_count
    names = jnp.where(live, tile_block[0], lax.axis_size("z")).astype(jnp.bfloat16)
    names = jnp.pad(names, ((0, 0), (0, LANES - slots)))
    names = jnp.broadcast_to(names, (NAME_ROWS, LANES))
    grams = exchange(first(names, pieces, peers), "x")
    wanted = grams[:, -1].astype(jnp.int32)
    factors = exchange(pick(wanted, pieces, grams, slots), "x")

    def reduce_rows(coded):
        return decode(exchange(coded, ITEMS), rows // owners, rank)

    right_side = reduce_rows(tile_sum(owners, tiles, factors))
    solution = jnp.zeros_like(right_side)
    residual = right_side
    direction = right_side
    norm_now = jnp.sum(residual * residual, axis=1, keepdims=True)
    for step in range(STEPS):
        left = gather(direction.astype(jnp.bfloat16), ITEMS).reshape(rows, rank)
        image = (
            reduce_rows(tile_sum(owners, tiles, factors, left))
            + DAMPING * direction
        )
        step_size = norm_now / jnp.sum(direction * image, axis=1, keepdims=True)
        solution = solution + step_size * direction
        residual = residual - step_size * image
        norm_next = jnp.sum(residual * residual, axis=1, keepdims=True)
        direction = residual + norm_next / norm_now * direction
        norm_now = norm_next
    return (solution, residual)


def solution(mesh):
    chips = Mesh(mesh.devices.reshape(8, 8, 8, 2), USERS + ITEMS)
    in_specs = (
        P(USERS, ITEMS, None, None, None),
        P(USERS, ITEMS, None),
        P(USERS, ITEMS),
        P(ITEMS + USERS, None),
    )
    out_specs = (P(USERS + ITEMS, None), P(USERS + ITEMS, None))
    return jax.shard_map(shards, mesh=chips, in_specs=in_specs, out_specs=out_specs, check_vma=False)
```

```python
import functools

import jax
import jax.numpy as jnp
from jax import lax
from jax.experimental import pallas as pl
from jax.experimental.pallas import tpu as pltpu
from jax.sharding import Mesh
from jax.sharding import PartitionSpec as P

STEPS = 2
DAMPING = 0.1
ROW_CHUNK = 256
VMEM_BYTES = 24 * 1024 * 1024
LANES = 128
SCALE_ROWS = 16
SENT_SCALE_ROWS = 8
NAME_ROWS = 16
SCALE_STEPS = 64.0
FULL_SCALE = 32000.0
USERS = ("z", "x")
ITEMS = ("y", "core")
WHOLE = pl.BlockSpec(memory_space=pltpu.VMEM)
SCALARS = pl.BlockSpec(memory_space=pltpu.SMEM)
FAR = pl.BlockSpec(memory_space=pltpu.HBM)


def first_kernel(names_ref, pieces_ref, out_ref):
    peers = out_ref.shape[0]
    rank = pieces_ref.shape[2]
    share = rank // peers
    strips = rank // LANES
    flat = pieces_ref[...].reshape(-1, rank)
    gram = lax.dot_general(
        flat, flat, (((0,), (0,)), ((), ())), preferred_element_type=jnp.float32
    ).astype(jnp.bfloat16)
    names = names_ref[...]
    for peer in range(peers):
        rows = gram[peer * share : (peer + 1) * share]
        for strip in range(strips):
            out_ref[peer, pl.ds(strip * share, share), :] = rows[
                :, strip * LANES : (strip + 1) * LANES
            ]
        out_ref[peer, pl.ds(strips * share, NAME_ROWS), :] = names


def first(names, pieces, peers):
    rank = pieces.shape[-1]
    return pl.pallas_call(
        first_kernel,
        out_shape=jax.ShapeDtypeStruct(
            (peers, rank // peers * rank // LANES + NAME_ROWS, LANES), pieces.dtype
        ),
        in_specs=[WHOLE, WHOLE],
        out_specs=WHOLE,
        compiler_params=pltpu.CompilerParams(vmem_limit_bytes=VMEM_BYTES),
    )(names, pieces)


def pick_kernel(wanted_ref, pieces_ref, grams_ref, out_ref):
    peers, height, rank = out_ref.shape
    share = rank // peers
    blocks, piece, _ = pieces_ref.shape
    slots = (height - share) // piece
    gram = jnp.concatenate(
        [
            jnp.sum(grams_ref[:, pl.ds(strip * share, share), :].astype(jnp.float32), axis=0)
            for strip in range(rank // LANES)
        ],
        axis=1,
    ).astype(jnp.bfloat16)
    for peer in range(peers):
        for slot in range(slots):
            name = wanted_ref[peer, slot]
            rows = pl.ds(slot * piece, piece)

            @pl.when(name < blocks)
            def live():
                out_ref[peer, rows, :] = pieces_ref[name]

            @pl.when(name >= blocks)
            def dead():
                out_ref[peer, rows, :] = jnp.zeros((piece, rank), out_ref.dtype)

        out_ref[peer, pl.ds(slots * piece, share), :] = gram


def pick(wanted, pieces, grams, slots):
    peers = wanted.shape[0]
    _, piece, rank = pieces.shape
    return pl.pallas_call(
        pick_kernel,
        out_shape=jax.ShapeDtypeStruct((peers, slots * piece + rank // peers, rank), pieces.dtype),
        in_specs=[SCALARS, WHOLE, WHOLE],
        out_specs=WHOLE,
        compiler_params=pltpu.CompilerParams(vmem_limit_bytes=VMEM_BYTES),
    )(wanted, pieces, grams)


def hold_kernel(tiles_ref, held_ref, arrived):
    copy = pltpu.make_async_copy(tiles_ref, held_ref, arrived)
    copy.start()
    copy.wait()


def hold(tiles):
    return pl.pallas_call(
        hold_kernel,
        out_shape=jax.ShapeDtypeStruct(tiles.shape, tiles.dtype),
        in_specs=[FAR],
        out_specs=WHOLE,
        scratch_shapes=[pltpu.SemaphoreType.DMA],
        compiler_params=pltpu.CompilerParams(vmem_limit_bytes=VMEM_BYTES),
        cost_estimate=pl.CostEstimate(flops=0, transcendentals=0, bytes_accessed=4 * tiles.size),
    )(tiles)


def tile_kernel(with_direction, tiles_ref, factors_ref, *refs):
    if with_direction:
        left_ref, out_ref, total_ref = refs
    else:
        out_ref, total_ref = refs
    slots = tiles_ref.shape[0]
    rows, rank = total_ref.shape
    piece = rows // factors_ref.shape[0]
    step = min(ROW_CHUNK, rows)
    if with_direction:
        share = factors_ref.shape[1] - slots * piece
        gram = factors_ref[:, pl.ds(slots * piece, share), :].reshape(rank, rank)
    for at in range(0, rows, step):
        chunk = pl.ds(at, step)
        if with_direction:
            left = left_ref[chunk, :]
            total = jnp.dot(left, gram, preferred_element_type=jnp.float32)
        else:
            total = jnp.zeros((step, rank), jnp.float32)
        for slot in range(slots):
            factors = factors_ref[:, pl.ds(slot * piece, piece), :].reshape(rows, rank)
            values = tiles_ref[slot, chunk, :].astype(jnp.float32)
            if with_direction:
                scores = lax.dot_general(
                    left, factors, (((1,), (1,)), ((), ())), preferred_element_type=jnp.float32
                )
                weighted = (values * scores).astype(jnp.bfloat16)
            else:
                weighted = (1.0 + values).astype(jnp.bfloat16)
            total += jnp.dot(weighted, factors, preferred_element_type=jnp.float32)
        total_ref[chunk, :] = total
    encode(total_ref, out_ref)


def encode(total_ref, out_ref):
    owners = out_ref.shape[0]
    share = total_ref.shape[0] // owners
    for owner in range(owners):
        block = total_ref[pl.ds(owner * share, share), :]
        largest = jnp.max(jnp.abs(block), axis=(0, 1), keepdims=True)
        level = jnp.ceil(jnp.log(jnp.maximum(largest, 1e-30)) * SCALE_STEPS)
        whole = jnp.round(block * (FULL_SCALE * jnp.exp(level * (-1.0 / SCALE_STEPS))))
        whole = whole.astype(jnp.int32).astype(jnp.int16)
        for at in range(0, block.shape[1], LANES):
            out_ref[owner, pl.ds(at // LANES * share, share), :] = whole[:, at : at + LANES]
        out_ref[owner, pl.ds(out_ref.shape[1] - SCALE_ROWS, SCALE_ROWS), :] = jnp.broadcast_to(
            level.astype(jnp.int32), (SCALE_ROWS, LANES)
        ).astype(jnp.int16)


def decode(parts, share, rank):
    levels = parts[:, -1:, :1].astype(jnp.float32)
    values = parts[:, : share * rank // LANES].astype(jnp.float32)
    total = jnp.sum(values * (jnp.exp(levels * (1.0 / SCALE_STEPS)) * (1.0 / FULL_SCALE)), axis=0)
    return jnp.concatenate([total[at : at + share] for at in range(0, total.shape[0], share)], axis=1)


def tile_sum(owners, tiles, factors, left=None):
    slots, rows, items = tiles.shape
    rank = factors.shape[-1]
    extra = () if left is None else (left,)
    return pl.pallas_call(
        functools.partial(tile_kernel, left is not None),
        out_shape=jax.ShapeDtypeStruct(
            (owners, rows // owners * rank // LANES + SCALE_ROWS, LANES), jnp.int16
        ),
        in_specs=[WHOLE, WHOLE] + [WHOLE] * len(extra),
        out_specs=WHOLE,
        scratch_shapes=[
            pltpu.VMEM((rows, rank), jnp.float32),
        ],
        compiler_params=pltpu.CompilerParams(vmem_limit_bytes=VMEM_BYTES),
    )(tiles, factors, *extra)


def exchange(parts, axes):
    return lax.all_to_all(parts, axes, 0, 0, tiled=True)


def gather(block, axes):
    size = lax.axis_size(axes)
    return exchange(jnp.broadcast_to(block[None], (size,) + block.shape), axes)


def shards(confidence, tile_block, tile_count, item_factors):
    tiles = hold(confidence[0, 0])
    slots, rows, _ = tiles.shape
    rank = item_factors.shape[1]
    owners = lax.axis_size(ITEMS)

    peers = lax.axis_size("x")
    pieces = gather(item_factors, "z")
    live = jnp.arange(slots, dtype=jnp.int32)[None] < tile_count
    names = jnp.where(live, tile_block[0], lax.axis_size("z")).astype(jnp.bfloat16)
    names = jnp.pad(names, ((0, 0), (0, LANES - slots)))
    names = jnp.broadcast_to(names, (NAME_ROWS, LANES))
    grams = exchange(first(names, pieces, peers), "x")
    wanted = grams[:, -1].astype(jnp.int32)
    factors = exchange(pick(wanted, pieces, grams, slots), "x")

    def reduce_rows(coded):
        sent = coded[:, : coded.shape[1] - SCALE_ROWS + SENT_SCALE_ROWS]
        return decode(exchange(sent, ITEMS), rows // owners, rank)

    right_side = reduce_rows(tile_sum(owners, tiles, factors))
    solution = jnp.zeros_like(right_side)
    residual = right_side
    direction = right_side
    norm_now = jnp.sum(residual * residual, axis=1, keepdims=True)
    for step in range(STEPS):
        left = gather(direction.astype(jnp.bfloat16), ITEMS).reshape(rows, rank)
        image = (
            reduce_rows(tile_sum(owners, tiles, factors, left))
            + DAMPING * direction
        )
        step_size = norm_now / jnp.sum(direction * image, axis=1, keepdims=True)
        solution = solution + step_size * direction
        residual = residual - step_size * image
        norm_next = jnp.sum(residual * residual, axis=1, keepdims=True)
        direction = residual + norm_next / norm_now * direction
        norm_now = norm_next
    return (solution, residual)


def solution(mesh):
    chips = Mesh(mesh.devices.reshape(8, 8, 8, 2), USERS + ITEMS)
    in_specs = (
        P(USERS, ITEMS, None, None, None),
        P(USERS, ITEMS, None),
        P(USERS, ITEMS),
        P(ITEMS + USERS, None),
    )
    out_specs = (P(USERS + ITEMS, None), P(USERS + ITEMS, None))
    return jax.shard_map(shards, mesh=chips, in_specs=in_specs, out_specs=out_specs, check_vma=False)
```

```python
import functools

import jax
import jax.numpy as jnp
from jax import lax
from jax.experimental import pallas as pl
from jax.experimental.pallas import tpu as pltpu
from jax.sharding import Mesh
from jax.sharding import PartitionSpec as P

STEPS = 2
DAMPING = 0.1
ROW_CHUNK = 256
VMEM_BYTES = 24 * 1024 * 1024
LANES = 128
SCALE_ROWS = 16
SENT_SCALE_ROWS = 8
NAME_ROWS = 16
SCALE_STEPS = 64.0
FULL_SCALE = 32000.0
USERS = ("z", "x")
ITEMS = ("y", "core")
WHOLE = pl.BlockSpec(memory_space=pltpu.VMEM)
SCALARS = pl.BlockSpec(memory_space=pltpu.SMEM)
FAR = pl.BlockSpec(memory_space=pltpu.HBM)


def first_kernel(names_ref, pieces_ref, out_ref):
    peers = out_ref.shape[0]
    rank = pieces_ref.shape[2]
    share = rank // peers
    strips = rank // LANES
    flat = pieces_ref[...].reshape(-1, rank)
    gram = lax.dot_general(
        flat, flat, (((0,), (0,)), ((), ())), preferred_element_type=jnp.float32
    ).astype(jnp.bfloat16)
    names = names_ref[...]
    for peer in range(peers):
        rows = gram[peer * share : (peer + 1) * share]
        for strip in range(strips):
            out_ref[peer, pl.ds(strip * share, share), :] = rows[
                :, strip * LANES : (strip + 1) * LANES
            ]
        out_ref[peer, pl.ds(strips * share, NAME_ROWS), :] = names


def first(names, pieces, peers):
    rank = pieces.shape[-1]
    return pl.pallas_call(
        first_kernel,
        out_shape=jax.ShapeDtypeStruct(
            (peers, rank // peers * rank // LANES + NAME_ROWS, LANES), pieces.dtype
        ),
        in_specs=[WHOLE, WHOLE],
        out_specs=WHOLE,
        compiler_params=pltpu.CompilerParams(vmem_limit_bytes=VMEM_BYTES),
    )(names, pieces)


def pick_kernel(wanted_ref, pieces_ref, grams_ref, out_ref):
    peers, height, rank = out_ref.shape
    share = rank // peers
    blocks, piece, _ = pieces_ref.shape
    slots = (height - share) // piece
    gram = jnp.concatenate(
        [
            jnp.sum(grams_ref[:, pl.ds(strip * share, share), :].astype(jnp.float32), axis=0)
            for strip in range(rank // LANES)
        ],
        axis=1,
    ).astype(jnp.bfloat16)
    for peer in range(peers):
        for slot in range(slots):
            name = wanted_ref[peer, slot]
            rows = pl.ds(slot * piece, piece)

            @pl.when(name < blocks)
            def live():
                out_ref[peer, rows, :] = pieces_ref[name]

            @pl.when(name >= blocks)
            def dead():
                out_ref[peer, rows, :] = jnp.zeros((piece, rank), out_ref.dtype)

        out_ref[peer, pl.ds(slots * piece, share), :] = gram


def pick(wanted, pieces, grams, slots):
    peers = wanted.shape[0]
    _, piece, rank = pieces.shape
    return pl.pallas_call(
        pick_kernel,
        out_shape=jax.ShapeDtypeStruct((peers, slots * piece + rank // peers, rank), pieces.dtype),
        in_specs=[SCALARS, WHOLE, WHOLE],
        out_specs=WHOLE,
        compiler_params=pltpu.CompilerParams(vmem_limit_bytes=VMEM_BYTES),
    )(wanted, pieces, grams)


def hold_kernel(tiles_ref, held_ref, arrived):
    copy = pltpu.make_async_copy(tiles_ref, held_ref, arrived)
    copy.start()
    copy.wait()


def hold(tiles):
    return pl.pallas_call(
        hold_kernel,
        out_shape=jax.ShapeDtypeStruct(tiles.shape, tiles.dtype),
        in_specs=[FAR],
        out_specs=WHOLE,
        scratch_shapes=[pltpu.SemaphoreType.DMA],
        compiler_params=pltpu.CompilerParams(vmem_limit_bytes=VMEM_BYTES),
        cost_estimate=pl.CostEstimate(flops=0, transcendentals=0, bytes_accessed=4 * tiles.size),
    )(tiles)


def tile_kernel(with_direction, tiles_ref, factors_ref, *refs):
    if with_direction:
        left_ref, out_ref, total_ref = refs
    else:
        out_ref, total_ref = refs
    slots = tiles_ref.shape[0]
    rows, rank = total_ref.shape
    piece = rows // factors_ref.shape[0]
    step = min(ROW_CHUNK, rows)
    if with_direction:
        share = factors_ref.shape[1] - slots * piece
        gram = factors_ref[:, pl.ds(slots * piece, share), :].reshape(rank, rank)
    for at in range(0, rows, step):
        chunk = pl.ds(at, step)
        if with_direction:
            left = left_ref[chunk, :]
            total = jnp.dot(left, gram, preferred_element_type=jnp.float32)
        else:
            total = jnp.zeros((step, rank), jnp.float32)
        for slot in range(slots):
            factors = factors_ref[:, pl.ds(slot * piece, piece), :].reshape(rows, rank)
            values = tiles_ref[slot, chunk, :].astype(jnp.float32)
            if with_direction:
                scores = lax.dot_general(
                    left, factors, (((1,), (1,)), ((), ())), preferred_element_type=jnp.float32
                )
                weighted = (values * scores).astype(jnp.bfloat16)
            else:
                weighted = (1.0 + values).astype(jnp.bfloat16)
            total += jnp.dot(weighted, factors, preferred_element_type=jnp.float32)
        total_ref[chunk, :] = total
    encode(total_ref, out_ref)


def encode(total_ref, out_ref):
    owners = out_ref.shape[0]
    share = total_ref.shape[0] // owners
    for owner in range(owners):
        block = total_ref[pl.ds(owner * share, share), :]
        largest = jnp.max(jnp.abs(block), axis=(0, 1), keepdims=True)
        level = jnp.ceil(jnp.log(jnp.maximum(largest, 1e-30)) * SCALE_STEPS)
        whole = jnp.round(block * (FULL_SCALE * jnp.exp(level * (-1.0 / SCALE_STEPS))))
        whole = whole.astype(jnp.int32).astype(jnp.int16)
        for at in range(0, block.shape[1], LANES):
            out_ref[owner, pl.ds(at // LANES * share, share), :] = whole[:, at : at + LANES]
        out_ref[owner, pl.ds(out_ref.shape[1] - SCALE_ROWS, SCALE_ROWS), :] = jnp.broadcast_to(
            level.astype(jnp.int32), (SCALE_ROWS, LANES)
        ).astype(jnp.int16)


def decode(parts, share, rank):
    levels = parts[:, -1:, :1].astype(jnp.float32)
    values = parts[:, : share * rank // LANES].astype(jnp.float32)
    total = jnp.sum(values * (jnp.exp(levels * (1.0 / SCALE_STEPS)) * (1.0 / FULL_SCALE)), axis=0)
    return jnp.concatenate([total[at : at + share] for at in range(0, total.shape[0], share)], axis=1)


def tile_sum(owners, tiles, factors, left=None):
    slots, rows, items = tiles.shape
    rank = factors.shape[-1]
    extra = () if left is None else (left,)
    return pl.pallas_call(
        functools.partial(tile_kernel, left is not None),
        out_shape=jax.ShapeDtypeStruct(
            (owners, rows // owners * rank // LANES + SCALE_ROWS, LANES), jnp.int16
        ),
        in_specs=[WHOLE, WHOLE] + [WHOLE] * len(extra),
        out_specs=WHOLE,
        scratch_shapes=[
            pltpu.VMEM((rows, rank), jnp.float32),
        ],
        compiler_params=pltpu.CompilerParams(vmem_limit_bytes=VMEM_BYTES),
    )(tiles, factors, *extra)


def exchange(parts, axes):
    return lax.all_to_all(parts, axes, 0, 0, tiled=True)


def gather(block, axes):
    size = lax.axis_size(axes)
    return exchange(jnp.broadcast_to(block[None], (size,) + block.shape), axes)


def shards(confidence, tile_block, tile_count, item_factors):
    tiles = hold(confidence[0, 0])
    slots, rows, _ = tiles.shape
    rank = item_factors.shape[1]
    owners = lax.axis_size(ITEMS)

    peers = lax.axis_size("x")
    pieces = gather(item_factors, "z")
    live = jnp.arange(slots, dtype=jnp.int32)[None] < tile_count
    names = jnp.where(live, tile_block[0], lax.axis_size("z")).astype(jnp.bfloat16)
    names = jnp.pad(names, ((0, 0), (0, LANES - slots)))
    names = jnp.broadcast_to(names, (NAME_ROWS, LANES))
    sent = first(names, pieces, peers)
    grams = exchange(sent[:, : sent.shape[1] - NAME_ROWS + SENT_SCALE_ROWS], "x")
    wanted = grams[:, -1].astype(jnp.int32)
    factors = exchange(pick(wanted, pieces, grams, slots), "x")

    def reduce_rows(coded):
        sent = coded[:, : coded.shape[1] - SCALE_ROWS + SENT_SCALE_ROWS]
        return decode(exchange(sent, ITEMS), rows // owners, rank)

    right_side = reduce_rows(tile_sum(owners, tiles, factors))
    solution = jnp.zeros_like(right_side)
    residual = right_side
    direction = right_side
    norm_now = jnp.sum(residual * residual, axis=1, keepdims=True)
    for step in range(STEPS):
        left = gather(direction.astype(jnp.bfloat16), ITEMS).reshape(rows, rank)
        image = (
            reduce_rows(tile_sum(owners, tiles, factors, left))
            + DAMPING * direction
        )
        step_size = norm_now / jnp.sum(direction * image, axis=1, keepdims=True)
        solution = solution + step_size * direction
        residual = residual - step_size * image
        norm_next = jnp.sum(residual * residual, axis=1, keepdims=True)
        direction = residual + norm_next / norm_now * direction
        norm_now = norm_next
    return (solution, residual)


def solution(mesh):
    chips = Mesh(mesh.devices.reshape(8, 8, 8, 2), USERS + ITEMS)
    in_specs = (
        P(USERS, ITEMS, None, None, None),
        P(USERS, ITEMS, None),
        P(USERS, ITEMS),
        P(ITEMS + USERS, None),
    )
    out_specs = (P(USERS + ITEMS, None), P(USERS + ITEMS, None))
    return jax.shard_map(shards, mesh=chips, in_specs=in_specs, out_specs=out_specs, check_vma=False)
```
